32 devices in a mesh: cuts: 2 (over x), section: 4 (over y, core), dp: 4 (over z).
Axes of the slice: x: 2, y: 2, z: 4, core: 2. Of those that a mesh axis runs over, the one named last changes fastest.
Arguments:
- activations: bfloat16 [2, 4, 1024, 4096], P('cuts', 'section', 'dp'), may hold values from -6 to 6
- upstream_grad: bfloat16 [2, 4, 1024, 4096], P('cuts', 'section', 'dp'), may hold values from -6 to 6
- routes: int32 [2, 4, 1024, 4], P('cuts', 'section', 'dp'), may hold values from 0 to 15, as said below
- router_probs: float32 [2, 4, 1024, 4], P('cuts', 'section', 'dp'), may hold values from 0.2 to 1
- gate_weight: bfloat16 [4, 5376, 4096], P('section', 'dp'), may hold values from -0.09375 to 0.09375
- up_weight: bfloat16 [4, 5376, 4096], P('section', 'dp'), may hold values from -0.09375 to 0.09375
- down_weight: bfloat16 [4, 5376, 4096], P('section', 'dp'), may hold values from -0.078125 to 0.078125
Outputs:
- grad_gate: bfloat16 [4, 5376, 4096], P('section', 'dp')
- grad_up: bfloat16 [4, 5376, 4096], P('section', 'dp')
- grad_down: bfloat16 [4, 5376, 4096], P('section', 'dp')
- prev_grad: bfloat16 [2, 4, 1024, 4096], P('cuts', 'section', 'dp')
The draws below stay inside these ranges and needn't reach their ends.
Inputs may be any that keep to these rules, and one draw needn't show every extreme that they name: `routes`: each token names 4 different experts. In every aligned block of 256 tokens of one replica and section, from 32 to 64 tokens name expert 0, and in every draw some block has exactly 64.
All inputs are finite; a program needn't handle non-finite values.
Results may differ from the reference program's by a relative error of at most 0.025.
Values may be sent and summed in bfloat16 or wider, within the bound.
A program may use at most 192 MiB of HBM per device.

```python
import jax
import jax.numpy as jnp
from jax import lax

D = 4096
FFW = 5376
EXPERTS = 16
TOP = 4
TOK_DEV = 256
CAP = 64
ROWS = 256
TOKENS = 1024
N_CUTS = 2
N_SECTION = 4
N_DP = 4


def draw_routes(key, part):
    blocks = N_CUTS * N_SECTION * N_DP
    key_count, key_full, key_rank, key_other, key_place = jax.random.split(key, 5)
    counts = jax.random.randint(key_count, (blocks,), CAP // 2, CAP + 1)
    fullest = jax.random.randint(key_full, (), 0, blocks)
    counts = jnp.where(jnp.arange(blocks) == fullest, CAP, counts)
    ranking = jax.vmap(lambda one_key: jax.random.permutation(one_key, TOK_DEV))(jax.random.split(key_rank, blocks))
    chosen = (ranking < counts[:, None]).reshape(-1)
    others = jax.vmap(lambda one_key: jax.random.permutation(one_key, EXPERTS - 1) + 1)(jax.random.split(key_other, blocks * TOK_DEV))
    others = others[:, :TOP]
    position = jax.random.randint(key_place, (blocks * TOK_DEV,), 0, TOP)
    put_zero = chosen[:, None] & (jnp.arange(TOP)[None, :] == position[:, None])
    expert_ids = jnp.where(put_zero, 0, others)
    return expert_ids.reshape(N_CUTS, N_SECTION, TOKENS, TOP).astype(jnp.int32)


def block_levels(own_key, shape, cuts, smallest, high):
    factor_of, own = 1.0, jax.random.fold_in(own_key, 6)
    for dim, blocks in cuts:
        draws = jnp.exp(jax.random.uniform(jax.random.fold_in(own, dim), (blocks,), jnp.float32, smallest / len(cuts), high / len(cuts)))
        factor_of = factor_of * jnp.repeat(draws, shape[dim] // blocks).reshape([-1 if axis == dim else 1 for axis in range(len(shape))])
    return factor_of


def scatter_about(rng, extent, width, most, shards=(), kind=jnp.bfloat16):
    values = jax.random.normal(rng, extent, jnp.float32) * width
    if len(shards) > 0:
        values = block_levels(rng, extent, shards, -0.22, 0.18) * values
    return jnp.clip(values, min=-most, max=most).astype(kind)


def setup_inputs(seed: int = 0) -> dict:
    keys = jax.random.split(jax.random.key(seed), 8)
    activations = scatter_about(keys[0], (N_CUTS, N_SECTION, TOKENS, D), 1.0, 6.0, ((0, 2), (1, 4), (2, 4)))
    upstream_grad = scatter_about(keys[1], (N_CUTS, N_SECTION, TOKENS, D), 1.0, 6.0, ((0, 2), (1, 4), (2, 4)))
    routes = draw_routes(jax.random.fold_in(keys[7], 71), 0)
    router_probs = jnp.clip(0.2 + 0.8 * jax.random.uniform(keys[3], (N_CUTS, N_SECTION, TOKENS, TOP), jnp.float32) ** block_levels(keys[3], (N_CUTS, N_SECTION, TOKENS, TOP), ((0, 2), (1, 4), (2, 4)), -0.2, 0.2), 0.2, 1.0)
    gate_weight = scatter_about(keys[4], (N_SECTION, FFW, D), D ** -0.5, 0.09375, ((0, 4), (1, 4)))
    up_weight = scatter_about(keys[5], (N_SECTION, FFW, D), D ** -0.5, 0.09375, ((0, 4), (1, 4)))
    down_weight = scatter_about(keys[6], (N_SECTION, FFW, D), FFW ** -0.5, 0.078125, ((0, 4), (1, 4)))
    return dict(activations=activations, upstream_grad=upstream_grad, routes=routes, router_probs=router_probs, gate_weight=gate_weight, up_weight=up_weight, down_weight=down_weight)


def make_picker(is_routed):
    blocks_routed = is_routed.reshape(N_DP, TOK_DEV)
    row_index = jnp.cumsum(blocks_routed.astype(jnp.int32), axis=1) - 1
    wanted = jnp.arange(CAP, dtype=jnp.int32)
    picker = (row_index[:, None, :] == wanted[None, :, None]) & blocks_routed[:, None, :]
    return picker.astype(jnp.float32)


def pick_rows(picker, values):
    blocks = values.astype(jnp.float32).reshape(N_DP, TOK_DEV, D)
    packed = jnp.einsum("nct,ntd->ncd", picker, blocks)
    return packed.reshape(ROWS, D).astype(jnp.bfloat16)


def slice_backward(activations, upstream, routes, probs, gate_w, up_w, down_w):
    expert_hits = routes == 0
    router_weight = jnp.sum(jnp.where(expert_hits, probs, jnp.float32(0.0)), axis=1)
    is_routed = jnp.any(expert_hits, axis=1)
    scaled = (router_weight[:, None] * upstream.astype(jnp.float32)).astype(jnp.bfloat16)
    picker = make_picker(is_routed)
    rows_acts = pick_rows(picker, activations)
    rows_grads = pick_rows(picker, scaled)
    gate_pre = jnp.dot(rows_acts, gate_w.T, preferred_element_type=jnp.float32)
    up_pre = jnp.dot(rows_acts, up_w.T, preferred_element_type=jnp.float32)
    sig_gate = jax.nn.sigmoid(gate_pre)
    silu_gate = gate_pre * sig_gate
    hidden = (silu_gate * up_pre).astype(jnp.bfloat16)
    hidden_grad = jnp.dot(rows_grads, down_w.T, preferred_element_type=jnp.float32)
    gate_grad = (hidden_grad * up_pre * sig_gate * (1.0 + gate_pre * (1.0 - sig_gate))).astype(jnp.bfloat16)
    up_grad = (hidden_grad * silu_gate).astype(jnp.bfloat16)
    down_part = jnp.dot(hidden.T, rows_grads, preferred_element_type=jnp.float32)
    gate_part = jnp.dot(gate_grad.T, rows_acts, preferred_element_type=jnp.float32)
    up_part = jnp.dot(up_grad.T, rows_acts, preferred_element_type=jnp.float32)
    hid_dev = FFW // N_DP
    gate_blocks = gate_grad.astype(jnp.float32).reshape(ROWS, N_DP, hid_dev)
    up_blocks = up_grad.astype(jnp.float32).reshape(ROWS, N_DP, hid_dev)
    gate_wblocks = gate_w.astype(jnp.float32).reshape(N_DP, hid_dev, D)
    up_wblocks = up_w.astype(jnp.float32).reshape(N_DP, hid_dev, D)
    terms = jnp.einsum("rnh,nhd->nrd", gate_blocks, gate_wblocks) + jnp.einsum("rnh,nhd->nrd", up_blocks, up_wblocks)
    terms = lax.optimization_barrier(terms.astype(jnp.bfloat16)).astype(jnp.float32)
    input_rows = jnp.sum(terms, axis=0).astype(jnp.bfloat16)
    back = jnp.einsum("nct,ncd->ntd", picker, input_rows.astype(jnp.float32).reshape(N_DP, CAP, D))
    token_grad = back.reshape(TOKENS, D).astype(jnp.bfloat16)
    return gate_part, up_part, down_part, token_grad


def reference(activations, upstream_grad, routes, router_probs, gate_weight, up_weight, down_weight):
    gate_out = []
    up_out = []
    down_out = []
    token_grads = [[None] * N_SECTION for replica in range(N_CUTS)]
    for section_id in range(N_SECTION):
        gate_total = jnp.zeros((FFW, D), jnp.float32)
        up_total = jnp.zeros((FFW, D), jnp.float32)
        down_total = jnp.zeros((FFW, D), jnp.float32)
        for replica in range(N_CUTS):
            gate_part, up_part, down_part, token_grad = slice_backward(
                activations[replica, section_id], upstream_grad[replica, section_id],
                routes[replica, section_id], router_probs[replica, section_id],
                gate_weight[section_id], up_weight[section_id], down_weight[section_id])
            parts = lax.optimization_barrier((gate_part.astype(jnp.bfloat16), up_part.astype(jnp.bfloat16), down_part.astype(jnp.bfloat16)))
            gate_total = gate_total + parts[0].astype(jnp.float32)
            up_total = up_total + parts[1].astype(jnp.float32)
            down_total = down_total + parts[2].astype(jnp.float32)
            token_grads[replica][section_id] = token_grad
        gate_out.append(gate_total.astype(jnp.bfloat16))
        up_out.append(up_total.astype(jnp.bfloat16))
        down_out.append(down_total.astype(jnp.bfloat16))
    zero_rows = jnp.zeros((TOKENS, D), jnp.bfloat16)
    received = []
    for replica in range(N_CUTS):
        row_list = []
        for section_id in range(N_SECTION):
            if section_id + 1 < N_SECTION:
                row_list.append(token_grads[replica][section_id + 1])
            else:
                row_list.append(zero_rows)
        received.append(jnp.stack(row_list, axis=0))
    prev_grad = jnp.stack(received, axis=0)
    return jnp.stack(gate_out, axis=0), jnp.stack(up_out, axis=0), jnp.stack(down_out, axis=0), prev_grad
```

```python
import jax
import jax.numpy as jnp
from jax import lax
from jax.sharding import PartitionSpec as P

CAP = 64


def from_behind(block, axis, distance):
    devices = range(lax.axis_size(axis))
    route = [(i - distance, i) for i in devices if i - distance in devices]
    return lax.ppermute(block, axis, route)


def contract_last(left, right):
    return lax.dot_general(
        left, right, (((1,), (1,)), ((), ())), preferred_element_type=jnp.float32
    )


def contract_first(left, right):
    return lax.dot_general(
        left, right, (((0,), (0,)), ((), ())), preferred_element_type=jnp.float32
    )


def hidden_backward(rows_acts, rows_grads, gate_local, up_local, down_local):
    gate_pre = contract_last(rows_acts, gate_local)
    up_pre = contract_last(rows_acts, up_local)
    sig_gate = jax.nn.sigmoid(gate_pre)
    silu_gate = gate_pre * sig_gate
    hidden = (silu_gate * up_pre).astype(jnp.bfloat16)
    hidden_grad = contract_last(rows_grads, down_local)
    gate_grad = (hidden_grad * up_pre * sig_gate * (1.0 + gate_pre * (1.0 - sig_gate))).astype(
        jnp.bfloat16
    )
    up_grad = (hidden_grad * silu_gate).astype(jnp.bfloat16)
    return hidden, gate_grad, up_grad


def per_device(
    activations, upstream_grad, routes, router_probs, gate_weight, up_weight, down_weight
):
    local_acts = activations[0, 0]
    local_grads = upstream_grad[0, 0]
    expert_hits = routes[0, 0] == 0
    router_weight = jnp.sum(jnp.where(expert_hits, router_probs[0, 0], jnp.float32(0.0)), axis=1)
    is_routed = jnp.any(expert_hits, axis=1)
    row_index = jnp.cumsum(is_routed.astype(jnp.int32)) - 1
    wanted = jnp.arange(CAP, dtype=jnp.int32)
    picker = ((row_index[None, :] == wanted[:, None]) & is_routed[None, :]).astype(jnp.bfloat16)
    scaled = (router_weight[:, None] * local_grads.astype(jnp.float32)).astype(jnp.bfloat16)
    packed_acts = jnp.dot(picker, local_acts, preferred_element_type=jnp.float32).astype(
        jnp.bfloat16
    )
    packed_grads = jnp.dot(picker, scaled, preferred_element_type=jnp.float32).astype(jnp.bfloat16)
    gate_local = gate_weight[0]
    up_local = up_weight[0]
    down_local = down_weight[0]
    rows_acts = lax.all_gather(packed_acts, "dp", axis=0, tiled=True)
    rows_grads = lax.all_gather(packed_grads, "dp", axis=0, tiled=True)
    both_acts = lax.all_gather(rows_acts, "cuts", axis=0, tiled=True)
    both_grads = lax.all_gather(rows_grads, "cuts", axis=0, tiled=True)
    _, gate_grad, up_grad = hidden_backward(
        rows_acts, rows_grads, gate_local, up_local, down_local
    )
    input_rows = lax.psum_scatter(
        (
            jnp.dot(gate_grad, gate_local, preferred_element_type=jnp.float32)
            + jnp.dot(up_grad, up_local, preferred_element_type=jnp.float32)
        ).astype(jnp.bfloat16),
        "dp",
        scatter_dimension=0,
        tiled=True,
    )
    hidden, gate_grad, up_grad = hidden_backward(
        both_acts, both_grads, gate_local, up_local, down_local
    )
    grad_gate = contract_first(gate_grad, both_acts).astype(jnp.bfloat16)[None]
    grad_up = contract_first(up_grad, both_acts).astype(jnp.bfloat16)[None]
    grad_down = contract_first(hidden, both_grads).astype(jnp.bfloat16)[None]
    slot = jnp.where(is_routed, row_index, -1).astype(jnp.bfloat16)
    behind_rows = from_behind(input_rows, "section", -1)
    behind_slot = from_behind(slot + 1.0, "section", -1) - 1.0
    behind_picker = (
        behind_slot[None, :].astype(jnp.int32) == wanted[:, None]
    ).astype(jnp.bfloat16)
    prev_grad = contract_first(behind_picker, behind_rows).astype(jnp.bfloat16)[None, None]
    return (grad_gate, grad_up, grad_down, prev_grad)


def solution(mesh):
    placed = (
        P("cuts", "section", "dp", None),
        P("cuts", "section", "dp", None),
        P("cuts", "section", "dp", None),
        P("cuts", "section", "dp", None),
        P("section", "dp", None),
        P("section", "dp", None),
        P("section", "dp", None),
    )
    return jax.shard_map(
        per_device,
        mesh=mesh,
        in_specs=placed,
        out_specs=(
            P("section", "dp", None),
            P("section", "dp", None),
            P("section", "dp", None),
            P("cuts", "section", "dp", None),
        ),
        check_vma=False,
    )
```

```python
import functools

import jax
import jax.numpy as jnp
from jax import lax
from jax.experimental import pallas as pl
from jax.experimental.pallas import tpu as pltpu
from jax.sharding import PartitionSpec as P

CAP = 64


def from_behind(block, axis, distance):
    devices = range(lax.axis_size(axis))
    route = [(i - distance, i) for i in devices if i - distance in devices]
    return lax.ppermute(block, axis, route)


def contract_last(left, right):
    return lax.dot_general(
        left, right, (((1,), (1,)), ((), ())), preferred_element_type=jnp.float32
    )


def contract_first(left, right):
    return lax.dot_general(
        left, right, (((0,), (0,)), ((), ())), preferred_element_type=jnp.float32
    )


def hidden_backward(rows_acts, rows_grads, gate_local, up_local, down_local):
    gate_pre = contract_last(rows_acts, gate_local)
    up_pre = contract_last(rows_acts, up_local)
    sig_gate = jax.nn.sigmoid(gate_pre)
    silu_gate = gate_pre * sig_gate
    hidden = (silu_gate * up_pre).astype(jnp.bfloat16)
    hidden_grad = contract_last(rows_grads, down_local)
    gate_grad = (hidden_grad * up_pre * sig_gate * (1.0 + gate_pre * (1.0 - sig_gate))).astype(
        jnp.bfloat16
    )
    up_grad = (hidden_grad * silu_gate).astype(jnp.bfloat16)
    return hidden, gate_grad, up_grad


TILES = 3
VMEM_BUDGET = 60 * 2**20


def exchange_kernel(
    n, acts_in, grads_in, gate_hbm, up_hbm, down_hbm,
    acts_out, grads_out, hidden_o, gate_o, up_o, input_o,
    acts_buf, grads_buf, gate_w, up_w, down_w, gate_t, up_t, part, from_low, from_high,
    own_sem, weight_sem, out_sem, z_recv, up_send, down_send, x_recv, x_send,
    low_recv, high_recv, sum_up_send, sum_down_send,
):
    i = lax.axis_index("dp")
    c = lax.axis_index("cuts")
    other = 1 - c
    cap = acts_in.shape[0]
    rows = n * cap
    hid, width = gate_w.shape
    tile = hid // TILES
    bufs = (acts_buf, grads_buf)
    has_low, has_high = i > 0, i < n - 1
    low, high, across = {"dp": i - 1}, {"dp": i + 1}, {"cuts": other}

    weight_copies = [
        pltpu.make_async_copy(src, dst, weight_sem.at[k])
        for k, (src, dst) in enumerate(
            ((gate_hbm, gate_w), (up_hbm, up_w), (down_hbm, down_w))
        )
    ]

    def slot(kind, replica, j):
        return bufs[kind].at[replica, pl.ds(pl.multiple_of(j * cap, cap), cap), :]

    own_copies = [
        pltpu.make_async_copy(src, slot(kind, c, i), own_sem.at[kind])
        for kind, src in enumerate((acts_in, grads_in))
    ]
    for copy in own_copies:
        copy.start()

    barrier = pltpu.get_barrier_semaphore()

    def greet(where):
        pl.semaphore_signal(
            barrier, inc=1, device_id=where, device_id_type=pl.DeviceIdType.MESH
        )

    pl.when(has_low)(lambda: greet(low))
    pl.when(has_high)(lambda: greet(high))
    greet(across)
    pl.semaphore_wait(barrier, 1 + jnp.int32(has_low) + jnp.int32(has_high))
    for copy in own_copies:
        copy.wait()

    def send(kind, j, where, send_sem, recv_sem):
        return pltpu.make_async_remote_copy(
            src_ref=slot(kind, c, j),
            dst_ref=slot(kind, c, j),
            send_sem=send_sem.at[kind, j],
            recv_sem=recv_sem.at[kind, j],
            device_id=where,
            device_id_type=pl.DeviceIdType.MESH,
        )

    def to_high(kind, j):
        return send(kind, j, high, up_send, z_recv)

    def to_low(kind, j):
        return send(kind, j, low, down_send, z_recv)

    def to_other(kind, j):
        return send(kind, j, across, x_send, x_recv)

    def from_other(kind, j):
        return pltpu.make_async_remote_copy(
            src_ref=slot(kind, other, j),
            dst_ref=slot(kind, other, j),
            send_sem=x_send.at[kind, j],
            recv_sem=x_recv.at[kind, j],
            device_id=across,
            device_id_type=pl.DeviceIdType.MESH,
        )

    for kind in range(2):
        pl.when(has_high)(lambda kind=kind: to_high(kind, i).start())
        pl.when(has_low)(lambda kind=kind: to_low(kind, i).start())
        to_other(kind, i).start()
    for copy in weight_copies:
        copy.start()
    for d in range(1, n):
        for kind in range(2):

            @pl.when(i - d >= 0)
            def _(kind=kind, d=d):
                to_high(kind, i - d).wait_recv()
                pl.when(has_high)(lambda: to_high(kind, i - d).start())
                to_other(kind, i - d).start()

            @pl.when(i + d < n)
            def _(kind=kind, d=d):
                to_low(kind, i + d).wait_recv()
                pl.when(has_low)(lambda: to_low(kind, i + d).start())
                to_other(kind, i + d).start()

    for copy in weight_copies:
        copy.wait()

    def forward(replica, t):
        some = pl.ds(pl.multiple_of(t * tile, tile), tile)
        cols = pl.ds(pl.multiple_of(replica * rows, rows), rows)
        acts = acts_buf[replica]
        gate_pre = contract_last(gate_w[some, :], acts)
        up_pre = contract_last(up_w[some, :], acts)
        hidden_grad = contract_last(down_w[some, :], grads_buf[replica])
        sig = jax.nn.sigmoid(gate_pre)
        silu = gate_pre * sig
        hidden_o[some, cols] = (silu * up_pre).astype(jnp.bfloat16)
        gate_o[some, cols] = (
            hidden_grad * up_pre * sig * (1.0 + gate_pre * (1.0 - sig))
        ).astype(jnp.bfloat16)
        up_o[some, cols] = (hidden_grad * silu).astype(jnp.bfloat16)

    @pl.loop(0, TILES)
    def _(t):
        forward(c, t)

    own_cols = pl.ds(pl.multiple_of(c * rows, rows), rows)
    gate_t[...] = jnp.transpose(gate_o[:, own_cols])
    up_t[...] = jnp.transpose(up_o[:, own_cols])
    step = 512

    @pl.loop(0, width // step)
    def _(t):
        some = pl.ds(pl.multiple_of(t * step, step), step)
        part[:, some] = (
            jnp.dot(gate_t[...], gate_w[:, some], preferred_element_type=jnp.float32)
            + jnp.dot(up_t[...], up_w[:, some], preferred_element_type=jnp.float32)
        ).astype(jnp.bfloat16)

    def share(j):
        return pl.ds(pl.multiple_of(j * cap, cap), cap)

    def sum_high(j):
        return pltpu.make_async_remote_copy(
            src_ref=part.at[share(j), :],
            dst_ref=from_low.at[j],
            send_sem=sum_up_send.at[j],
            recv_sem=low_recv.at[j],
            device_id=high,
            device_id_type=pl.DeviceIdType.MESH,
        )

    def sum_low(j):
        return pltpu.make_async_remote_copy(
            src_ref=part.at[share(j), :],
            dst_ref=from_high.at[j],
            send_sem=sum_down_send.at[j],
            recv_sem=high_recv.at[j],
            device_id=low,
            device_id_type=pl.DeviceIdType.MESH,
        )

    def add_to_part(arrived, j):
        part[share(j), :] = (
            part[share(j), :].astype(jnp.float32) + arrived[j].astype(jnp.float32)
        ).astype(jnp.bfloat16)

    def pass_up(j):
        @pl.when(i < j)
        def _():
            @pl.when(has_low)
            def _():
                sum_high(j).wait_recv()
                add_to_part(from_low, j)

            sum_high(j).start()

    def pass_down(j):
        @pl.when(i > j)
        def _():
            @pl.when(has_high)
            def _():
                sum_low(j).wait_recv()
                add_to_part(from_high, j)

            sum_low(j).start()

    lower_half = 2 * i < n
    for k in range(n - 1):

        @pl.when(lower_half)
        def _(k=k):
            pass_up(n - 1 - k)
            pass_down(k)

        @pl.when(jnp.logical_not(lower_half))
        def _(k=k):
            pass_down(k)
            pass_up(n - 1 - k)

        if k == 0:
            for j in range(n):
                for kind in range(2):
                    from_other(kind, j).wait_recv()
            out_copies = [
                pltpu.make_async_copy(acts_buf, acts_out, out_sem.at[0]),
                pltpu.make_async_copy(grads_buf, grads_out, out_sem.at[1]),
            ]
            for copy in out_copies:
                copy.start()
        if k < TILES:
            forward(other, k)
    for k in range(n - 1, TILES):
        forward(other, k)

    total = part[share(i), :].astype(jnp.float32)
    input_o[...] = total

    @pl.when(has_low)
    def _():
        sum_high(i).wait_recv()
        input_o[...] += from_low[i].astype(jnp.float32)

    @pl.when(has_high)
    def _():
        sum_low(i).wait_recv()
        input_o[...] += from_high[i].astype(jnp.float32)

    for j in range(n):
        pl.when(i < j)(lambda j=j: sum_high(j).wait_send())
        pl.when(i > j)(lambda j=j: sum_low(j).wait_send())
        for kind in range(2):
            to_other(kind, j).wait_send()
            pl.when(jnp.logical_and(has_high, i >= j))(
                lambda kind=kind, j=j: to_high(kind, j).wait_send()
            )
            pl.when(jnp.logical_and(has_low, i <= j))(
                lambda kind=kind, j=j: to_low(kind, j).wait_send()
            )
    for copy in out_copies:
        copy.wait()


def kernel_bytes(n, cap, hid, width):
    weights = 3 * hid * width * 2
    rows = 4 * n * cap * width * 2
    hidden = (6 + 2) * hid * n * cap * 2
    sums = 3 * n * cap * width * 2 + cap * width * 4
    return weights + rows + hidden + sums


def exchange(n, acts, grads, gate_local, up_local, down_local):
    cap, width = acts.shape
    hid = gate_local.shape[0]
    rows = n * cap
    bf16 = jnp.bfloat16
    both = jax.ShapeDtypeStruct((2, rows, width), bf16)
    units = jax.ShapeDtypeStruct((hid, 2 * rows), bf16)
    anywhere = pl.BlockSpec(memory_space=pl.ANY)
    vmem = pl.BlockSpec(memory_space=pltpu.VMEM)
    dma = pltpu.SemaphoreType.DMA
    return pl.pallas_call(
        functools.partial(exchange_kernel, n),
        out_shape=[both, both, units, units, units,
                   jax.ShapeDtypeStruct((cap, width), jnp.float32)],
        in_specs=[anywhere] * 5,
        out_specs=[anywhere, anywhere, vmem, vmem, vmem, vmem],
        scratch_shapes=[
            pltpu.VMEM((2, rows, width), bf16),
            pltpu.VMEM((2, rows, width), bf16),
            pltpu.VMEM((hid, width), bf16),
            pltpu.VMEM((hid, width), bf16),
            pltpu.VMEM((hid, width), bf16),
            pltpu.VMEM((rows, hid), bf16),
            pltpu.VMEM((rows, hid), bf16),
            pltpu.VMEM((rows, width), bf16),
            pltpu.VMEM((n, cap, width), bf16),
            pltpu.VMEM((n, cap, width), bf16),
            dma((2,)), dma((3,)), dma((2,)),
            dma((2, n)), dma((2, n)), dma((2, n)), dma((2, n)), dma((2, n)),
            dma((n,)), dma((n,)), dma((n,)), dma((n,)),
        ],
        compiler_params=pltpu.CompilerParams(
            collective_id=0, has_side_effects=True, vmem_limit_bytes=VMEM_BUDGET
        ),
        cost_estimate=pl.CostEstimate(
            flops=16 * rows * hid * width, bytes_accessed=8 * hid * width, transcendentals=0
        ),
    )(acts, grads, gate_local, up_local, down_local)


def per_device(
    activations, upstream_grad, routes, router_probs, gate_weight, up_weight, down_weight
):
    local_acts = activations[0, 0]
    local_grads = upstream_grad[0, 0]
    expert_hits = routes[0, 0] == 0
    router_weight = jnp.sum(jnp.where(expert_hits, router_probs[0, 0], jnp.float32(0.0)), axis=1)
    is_routed = jnp.any(expert_hits, axis=1)
    row_index = jnp.cumsum(is_routed.astype(jnp.int32)) - 1
    wanted = jnp.arange(CAP, dtype=jnp.int32)
    picker = ((row_index[None, :] == wanted[:, None]) & is_routed[None, :]).astype(jnp.bfloat16)
    scaled = (router_weight[:, None] * local_grads.astype(jnp.float32)).astype(jnp.bfloat16)
    packed_acts = jnp.dot(picker, local_acts, preferred_element_type=jnp.float32).astype(
        jnp.bfloat16
    )
    packed_grads = jnp.dot(picker, scaled, preferred_element_type=jnp.float32).astype(jnp.bfloat16)
    gate_local = gate_weight[0]
    up_local = up_weight[0]
    down_local = down_weight[0]
    n = lax.axis_size("dp")
    hid, width = gate_local.shape
    if kernel_bytes(n, CAP, hid, width) <= VMEM_BUDGET and hid % (16 * TILES) == 0:
        acts, grads, hidden, gate_grad, up_grad, input_rows = exchange(
            n, packed_acts, packed_grads, gate_local, up_local, down_local
        )
        input_rows = input_rows.astype(jnp.bfloat16)
        both_acts = acts.reshape(2 * n * CAP, width)
        both_grads = grads.reshape(2 * n * CAP, width)
        summed = functools.partial(jnp.dot, preferred_element_type=jnp.float32)
    else:
        rows_acts = lax.all_gather(packed_acts, "dp", axis=0, tiled=True)
        rows_grads = lax.all_gather(packed_grads, "dp", axis=0, tiled=True)
        both_acts = lax.all_gather(rows_acts, "cuts", axis=0, tiled=True)
        both_grads = lax.all_gather(rows_grads, "cuts", axis=0, tiled=True)
        _, gate_grad, up_grad = hidden_backward(
            rows_acts, rows_grads, gate_local, up_local, down_local
        )
        input_rows = lax.psum_scatter(
            (
                jnp.dot(gate_grad, gate_local, preferred_element_type=jnp.float32)
                + jnp.dot(up_grad, up_local, preferred_element_type=jnp.float32)
            ).astype(jnp.bfloat16),
            "dp",
            scatter_dimension=0,
            tiled=True,
        )
        hidden, gate_grad, up_grad = hidden_backward(
            both_acts, both_grads, gate_local, up_local, down_local
        )
        summed = contract_first
    grad_gate = summed(gate_grad, both_acts).astype(jnp.bfloat16)[None]
    grad_up = summed(up_grad, both_acts).astype(jnp.bfloat16)[None]
    grad_down = summed(hidden, both_grads).astype(jnp.bfloat16)[None]
    slot = jnp.where(is_routed, row_index, -1).astype(jnp.bfloat16)
    behind_rows = from_behind(input_rows, "section", -1)
    behind_slot = from_behind(slot + 1.0, "section", -1) - 1.0
    behind_picker = (
        behind_slot[None, :].astype(jnp.int32) == wanted[:, None]
    ).astype(jnp.bfloat16)
    prev_grad = contract_first(behind_picker, behind_rows).astype(jnp.bfloat16)[None, None]
    return (grad_gate, grad_up, grad_down, prev_grad)


def solution(mesh):
    placed = (
        P("cuts", "section", "dp", None),
        P("cuts", "section", "dp", None),
        P("cuts", "section", "dp", None),
        P("cuts", "section", "dp", None),
        P("section", "dp", None),
        P("section", "dp", None),
        P("section", "dp", None),
    )
    return jax.shard_map(
        per_device,
        mesh=mesh,
        in_specs=placed,
        out_specs=(
            P("section", "dp", None),
            P("section", "dp", None),
            P("section", "dp", None),
            P("cuts", "section", "dp", None),
        ),
        check_vma=False,
    )
```

```python
import functools

import jax
import jax.numpy as jnp
from jax import lax
from jax.experimental import pallas as pl
from jax.experimental.pallas import tpu as pltpu
from jax.sharding import PartitionSpec as P

CAP = 64


def from_behind(block, axis, distance):
    devices = range(lax.axis_size(axis))
    route = [(i - distance, i) for i in devices if i - distance in devices]
    return lax.ppermute(block, axis, route)


def contract_last(left, right):
    return lax.dot_general(
        left, right, (((1,), (1,)), ((), ())), preferred_element_type=jnp.float32
    )


def contract_first(left, right):
    return lax.dot_general(
        left, right, (((0,), (0,)), ((), ())), preferred_element_type=jnp.float32
    )


def hidden_backward(rows_acts, rows_grads, gate_local, up_local, down_local):
    gate_pre = contract_last(rows_acts, gate_local)
    up_pre = contract_last(rows_acts, up_local)
    sig_gate = jax.nn.sigmoid(gate_pre)
    silu_gate = gate_pre * sig_gate
    hidden = (silu_gate * up_pre).astype(jnp.bfloat16)
    hidden_grad = contract_last(rows_grads, down_local)
    gate_grad = (hidden_grad * up_pre * sig_gate * (1.0 + gate_pre * (1.0 - sig_gate))).astype(
        jnp.bfloat16
    )
    up_grad = (hidden_grad * silu_gate).astype(jnp.bfloat16)
    return hidden, gate_grad, up_grad


TILES = 3
VMEM_BUDGET = 60 * 2**20


def exchange_kernel(
    n, acts_in, grads_in, gate_hbm, up_hbm, down_hbm,
    acts_out, grads_out, hidden_o, gate_o, up_o, part, next_up, next_down,
    acts_buf, grads_buf, gate_w, up_w, down_w, gate_t, up_t, from_low, from_high,
    own_sem, weight_sem, out_sem, z_recv, up_send, down_send, x_recv, x_send,
    relay_send, low_recv, high_recv, sum_up_send, sum_down_send,
):
    i = lax.axis_index("dp")
    c = lax.axis_index("cuts")
    other = 1 - c
    cap = acts_in.shape[0]
    rows = n * cap
    hid, width = gate_w.shape
    tile = hid // TILES
    bufs = (acts_buf, grads_buf)
    has_low, has_high = i > 0, i < n - 1
    first, last = i == 0, i == n - 1
    second, next_last = i == 1, i == n - 2
    low, high, across = {"dp": i - 1}, {"dp": i + 1}, {"cuts": other}

    weight_copies = [
        pltpu.make_async_copy(src, dst, weight_sem.at[k])
        for k, (src, dst) in enumerate(
            ((gate_hbm, gate_w), (up_hbm, up_w), (down_hbm, down_w))
        )
    ]

    def slot(kind, replica, j):
        return bufs[kind].at[replica, pl.ds(pl.multiple_of(j * cap, cap), cap), :]

    own_copies = [
        pltpu.make_async_copy(src, slot(kind, c, i), own_sem.at[kind])
        for kind, src in enumerate((acts_in, grads_in))
    ]
    for copy in own_copies:
        copy.start()

    barrier = pltpu.get_barrier_semaphore()

    def greet(where):
        pl.semaphore_signal(
            barrier, inc=1, device_id=where, device_id_type=pl.DeviceIdType.MESH
        )

    pl.when(has_low)(lambda: greet(low))
    pl.when(has_high)(lambda: greet(high))
    greet(across)
    pl.semaphore_wait(barrier, 1 + jnp.int32(has_low) + jnp.int32(has_high))
    for copy in own_copies:
        copy.wait()

    def send(kind, j, where, send_sem, recv_sem):
        return pltpu.make_async_remote_copy(
            src_ref=slot(kind, c, j),
            dst_ref=slot(kind, c, j),
            send_sem=send_sem.at[kind, j],
            recv_sem=recv_sem.at[kind, j],
            device_id=where,
            device_id_type=pl.DeviceIdType.MESH,
        )

    def to_high(kind, j):
        return send(kind, j, high, up_send, z_recv)

    def to_low(kind, j):
        return send(kind, j, low, down_send, z_recv)

    def to_other(kind, j):
        return send(kind, j, across, x_send, x_recv)

    def from_other(kind, j):
        return pltpu.make_async_remote_copy(
            src_ref=slot(kind, other, j),
            dst_ref=slot(kind, other, j),
            send_sem=x_send.at[kind, j],
            recv_sem=x_recv.at[kind, j],
            device_id=across,
            device_id_type=pl.DeviceIdType.MESH,
        )

    def relay(kind, j, where):
        return pltpu.make_async_remote_copy(
            src_ref=slot(kind, other, j),
            dst_ref=slot(kind, other, j),
            send_sem=relay_send.at[kind],
            recv_sem=x_recv.at[kind, j],
            device_id=where,
            device_id_type=pl.DeviceIdType.MESH,
        )

    def crosses(kind, d):
        if d == 1:
            relayed = jnp.logical_or(second, last) if kind else second
            return jnp.logical_not(relayed)
        if d == -1:
            relayed = jnp.logical_or(next_last, first) if kind else next_last
            return jnp.logical_not(relayed)
        return i >= 0

    for kind in range(2):
        pl.when(has_high)(lambda kind=kind: to_high(kind, i).start())
        pl.when(has_low)(lambda kind=kind: to_low(kind, i).start())
        to_other(kind, i).start()
    for copy in weight_copies:
        copy.start()
    for d in range(1, n):
        for kind in range(2):

            @pl.when(i - d >= 0)
            def _(kind=kind, d=d):
                to_high(kind, i - d).wait_recv()
                pl.when(has_high)(lambda: to_high(kind, i - d).start())
                pl.when(crosses(kind, d))(lambda: to_other(kind, i - d).start())

            @pl.when(i + d < n)
            def _(kind=kind, d=d):
                to_low(kind, i + d).wait_recv()
                pl.when(has_low)(lambda: to_low(kind, i + d).start())
                pl.when(crosses(kind, -d))(lambda: to_other(kind, i + d).start())

        if d == 1:

            @pl.when(first)
            def _():
                for kind in range(2):
                    from_other(kind, 0).wait_recv()
                    relay(kind, 0, high).start()

            @pl.when(last)
            def _():
                for kind in range(2):
                    from_other(kind, n - 1).wait_recv()
                    relay(kind, n - 1, low).start()

    for copy in weight_copies:
        copy.wait()

    def forward(replica, t):
        some = pl.ds(pl.multiple_of(t * tile, tile), tile)
        cols = pl.ds(pl.multiple_of(replica * rows, rows), rows)
        acts = acts_buf[replica]
        gate_pre = contract_last(gate_w[some, :], acts)
        up_pre = contract_last(up_w[some, :], acts)
        hidden_grad = contract_last(down_w[some, :], grads_buf[replica])
        sig = jax.nn.sigmoid(gate_pre)
        silu = gate_pre * sig
        hidden_o[some, cols] = (silu * up_pre).astype(jnp.bfloat16)
        gate_o[some, cols] = (
            hidden_grad * up_pre * sig * (1.0 + gate_pre * (1.0 - sig))
        ).astype(jnp.bfloat16)
        up_o[some, cols] = (hidden_grad * silu).astype(jnp.bfloat16)

    @pl.loop(0, TILES)
    def _(t):
        forward(c, t)

    own_cols = pl.ds(pl.multiple_of(c * rows, rows), rows)
    gate_t[...] = jnp.transpose(gate_o[:, own_cols])
    up_t[...] = jnp.transpose(up_o[:, own_cols])
    step = 512

    @pl.loop(0, width // step)
    def _(t):
        some = pl.ds(pl.multiple_of(t * step, step), step)
        part[:, some] = (
            jnp.dot(gate_t[...], gate_w[:, some], preferred_element_type=jnp.float32)
            + jnp.dot(up_t[...], up_w[:, some], preferred_element_type=jnp.float32)
        ).astype(jnp.bfloat16)

    def share(j):
        return pl.ds(pl.multiple_of(j * cap, cap), cap)

    def sum_high():
        return pltpu.make_async_remote_copy(
            src_ref=part.at[share(n - 1), :],
            dst_ref=from_low,
            send_sem=sum_up_send,
            recv_sem=low_recv,
            device_id=high,
            device_id_type=pl.DeviceIdType.MESH,
        )

    def sum_low():
        return pltpu.make_async_remote_copy(
            src_ref=part.at[share(0), :],
            dst_ref=from_high,
            send_sem=sum_down_send,
            recv_sem=high_recv,
            device_id=low,
            device_id_type=pl.DeviceIdType.MESH,
        )

    pl.when(first)(lambda: sum_high().start())
    pl.when(last)(lambda: sum_low().start())

    @pl.when(second)
    def _():
        to_low(1, n - 1).wait_send()
        from_other(1, 1).wait_recv()
        relay(1, 1, low).start()

    @pl.when(next_last)
    def _():
        to_high(1, 0).wait_send()
        from_other(1, n - 2).wait_recv()
        relay(1, n - 2, high).start()

    for j in range(n):
        for kind in range(2):
            seen = []
            if j == 0:
                seen.append(first)
            if j == n - 1:
                seen.append(last)
            if kind == 1 and j == 1:
                seen.append(second)
            if kind == 1 and j == n - 2:
                seen.append(next_last)
            if seen:
                pl.when(jnp.logical_not(functools.reduce(jnp.logical_or, seen)))(
                    lambda kind=kind, j=j: from_other(kind, j).wait_recv()
                )
            else:
                from_other(kind, j).wait_recv()
    out_copies = [
        pltpu.make_async_copy(acts_buf, acts_out, out_sem.at[0]),
        pltpu.make_async_copy(grads_buf, grads_out, out_sem.at[1]),
    ]
    for copy in out_copies:
        copy.start()

    @pl.loop(0, TILES)
    def _(t):
        forward(other, t)

    next_up[...] = part[share(lax.rem(i + n - 2, n)), :]
    next_down[...] = part[share(lax.rem(i + 2, n)), :]

    @pl.when(second)
    def _():
        sum_high().wait_recv()
        next_up[...] = (
            next_up[...].astype(jnp.float32) + from_low[...].astype(jnp.float32)
        ).astype(jnp.bfloat16)

    @pl.when(next_last)
    def _():
        sum_low().wait_recv()
        next_down[...] = (
            next_down[...].astype(jnp.float32) + from_high[...].astype(jnp.float32)
        ).astype(jnp.bfloat16)

    pl.when(first)(lambda: sum_high().wait_send())
    pl.when(last)(lambda: sum_low().wait_send())

    @pl.when(first)
    def _():
        for kind in range(2):
            relay(kind, 0, high).wait_send()

    @pl.when(last)
    def _():
        for kind in range(2):
            relay(kind, n - 1, low).wait_send()

    pl.when(second)(lambda: relay(1, 1, low).wait_send())
    pl.when(next_last)(lambda: relay(1, n - 2, high).wait_send())
    for kind in range(2):
        to_other(kind, i).wait_send()
        pl.when(has_high)(lambda kind=kind: to_high(kind, i).wait_send())
        pl.when(has_low)(lambda kind=kind: to_low(kind, i).wait_send())
    for d in range(1, n):
        for kind in range(2):

            @pl.when(i - d >= 0)
            def _(kind=kind, d=d):
                early = jnp.logical_and(next_last, jnp.bool_(kind == 1 and d == n - 2))
                pl.when(jnp.logical_and(has_high, jnp.logical_not(early)))(
                    lambda: to_high(kind, i - d).wait_send()
                )
                pl.when(crosses(kind, d))(lambda: to_other(kind, i - d).wait_send())

            @pl.when(i + d < n)
            def _(kind=kind, d=d):
                early = jnp.logical_and(second, jnp.bool_(kind == 1 and d == n - 2))
                pl.when(jnp.logical_and(has_low, jnp.logical_not(early)))(
                    lambda: to_low(kind, i + d).wait_send()
                )
                pl.when(crosses(kind, -d))(lambda: to_other(kind, i + d).wait_send())

    for copy in out_copies:
        copy.wait()


def kernel_bytes(n, cap, hid, width):
    weights = 3 * hid * width * 2
    rows = 4 * n * cap * width * 2
    hidden = (6 + 2) * hid * n * cap * 2
    sums = 3 * n * cap * width * 2 + cap * width * 4
    return weights + rows + hidden + sums


def exchange(n, acts, grads, gate_local, up_local, down_local):
    cap, width = acts.shape
    hid = gate_local.shape[0]
    rows = n * cap
    bf16 = jnp.bfloat16
    both = jax.ShapeDtypeStruct((2, rows, width), bf16)
    units = jax.ShapeDtypeStruct((hid, 2 * rows), bf16)
    anywhere = pl.BlockSpec(memory_space=pl.ANY)
    vmem = pl.BlockSpec(memory_space=pltpu.VMEM)
    dma = pltpu.SemaphoreType.DMA
    return pl.pallas_call(
        functools.partial(exchange_kernel, n),
        out_shape=[both, both, units, units, units,
                   jax.ShapeDtypeStruct((rows, width), bf16),
                   jax.ShapeDtypeStruct((cap, width), bf16),
                   jax.ShapeDtypeStruct((cap, width), bf16)],
        in_specs=[anywhere] * 5,
        out_specs=[anywhere, anywhere] + [vmem] * 6,
        scratch_shapes=[
            pltpu.VMEM((2, rows, width), bf16),
            pltpu.VMEM((2, rows, width), bf16),
            pltpu.VMEM((hid, width), bf16),
            pltpu.VMEM((hid, width), bf16),
            pltpu.VMEM((hid, width), bf16),
            pltpu.VMEM((rows, hid), bf16),
            pltpu.VMEM((rows, hid), bf16),
            pltpu.VMEM((cap, width), bf16),
            pltpu.VMEM((cap, width), bf16),
            dma((2,)), dma((3,)), dma((2,)),
            dma((2, n)), dma((2, n)), dma((2, n)), dma((2, n)), dma((2, n)),
            dma((2,)), dma, dma, dma, dma,
        ],
        compiler_params=pltpu.CompilerParams(
            collective_id=0, has_side_effects=True, vmem_limit_bytes=VMEM_BUDGET
        ),
        cost_estimate=pl.CostEstimate(
            flops=16 * rows * hid * width, bytes_accessed=8 * hid * width, transcendentals=0
        ),
    )(acts, grads, gate_local, up_local, down_local)


def chained_sum(n, part, up, down):
    i = lax.axis_index("dp")
    sections = range(lax.axis_size("section"))
    shares = part.reshape(n, CAP, part.shape[1])

    def mine(j):
        return lax.dynamic_index_in_dim(shares, jnp.clip(j, 0, n - 1), keepdims=False)

    def hop(block, senders, step, back):
        pairs = [
            (s * n + k, (s - back) * n + k + step)
            for s in sections
            for k in senders
            if s >= back
        ]
        return lax.ppermute(block, ("section", "dp"), pairs)

    def joined(left, right):
        return (left.astype(jnp.float32) + right.astype(jnp.float32)).astype(jnp.bfloat16)

    for t in range(2, n):
        if t > 2:
            up = joined(up, mine(i + n - t))
            down = joined(down, mine(i - n + t))
        back = int(t == n - 1)
        up = hop(up, range(t), 1, back)
        down = hop(down, range(n - t, n), -1, back)
    own = hop(mine(i), range(n), 0, 1)
    total = own.astype(jnp.float32) + up.astype(jnp.float32) + down.astype(jnp.float32)
    return total.astype(jnp.bfloat16)


def per_device(
    activations, upstream_grad, routes, router_probs, gate_weight, up_weight, down_weight
):
    local_acts = activations[0, 0]
    local_grads = upstream_grad[0, 0]
    expert_hits = routes[0, 0] == 0
    router_weight = jnp.sum(jnp.where(expert_hits, router_probs[0, 0], jnp.float32(0.0)), axis=1)
    is_routed = jnp.any(expert_hits, axis=1)
    row_index = jnp.cumsum(is_routed.astype(jnp.int32)) - 1
    wanted = jnp.arange(CAP, dtype=jnp.int32)
    picker = ((row_index[None, :] == wanted[:, None]) & is_routed[None, :]).astype(jnp.bfloat16)
    scaled = (router_weight[:, None] * local_grads.astype(jnp.float32)).astype(jnp.bfloat16)
    packed_acts = jnp.dot(picker, local_acts, preferred_element_type=jnp.float32).astype(
        jnp.bfloat16
    )
    packed_grads = jnp.dot(picker, scaled, preferred_element_type=jnp.float32).astype(jnp.bfloat16)
    gate_local = gate_weight[0]
    up_local = up_weight[0]
    down_local = down_weight[0]
    n = lax.axis_size("dp")
    hid, width = gate_local.shape
    if kernel_bytes(n, CAP, hid, width) <= VMEM_BUDGET and hid % (16 * TILES) == 0 and n >= 4:
        acts, grads, hidden, gate_grad, up_grad, part, next_up, next_down = exchange(
            n, packed_acts, packed_grads, gate_local, up_local, down_local
        )
        behind_rows = chained_sum(n, part, next_up, next_down)
        both_acts = acts.reshape(2 * n * CAP, width)
        both_grads = grads.reshape(2 * n * CAP, width)
        summed = functools.partial(jnp.dot, preferred_element_type=jnp.float32)
    else:
        rows_acts = lax.all_gather(packed_acts, "dp", axis=0, tiled=True)
        rows_grads = lax.all_gather(packed_grads, "dp", axis=0, tiled=True)
        both_acts = lax.all_gather(rows_acts, "cuts", axis=0, tiled=True)
        both_grads = lax.all_gather(rows_grads, "cuts", axis=0, tiled=True)
        _, gate_grad, up_grad = hidden_backward(
            rows_acts, rows_grads, gate_local, up_local, down_local
        )
        input_rows = lax.psum_scatter(
            (
                jnp.dot(gate_grad, gate_local, preferred_element_type=jnp.float32)
                + jnp.dot(up_grad, up_local, preferred_element_type=jnp.float32)
            ).astype(jnp.bfloat16),
            "dp",
            scatter_dimension=0,
            tiled=True,
        )
        hidden, gate_grad, up_grad = hidden_backward(
            both_acts, both_grads, gate_local, up_local, down_local
        )
        behind_rows = from_behind(input_rows, "section", -1)
        summed = contract_first
    grad_gate = summed(gate_grad, both_acts).astype(jnp.bfloat16)[None]
    grad_up = summed(up_grad, both_acts).astype(jnp.bfloat16)[None]
    grad_down = summed(hidden, both_grads).astype(jnp.bfloat16)[None]
    slot = jnp.where(is_routed, row_index, -1).astype(jnp.bfloat16)
    behind_slot = from_behind(slot + 1.0, "section", -1) - 1.0
    behind_picker = (
        behind_slot[None, :].astype(jnp.int32) == wanted[:, None]
    ).astype(jnp.bfloat16)
    prev_grad = contract_first(behind_picker, behind_rows).astype(jnp.bfloat16)[None, None]
    return (grad_gate, grad_up, grad_down, prev_grad)


def solution(mesh):
    placed = (
        P("cuts", "section", "dp", None),
        P("cuts", "section", "dp", None),
        P("cuts", "section", "dp", None),
        P("cuts", "section", "dp", None),
        P("section", "dp", None),
        P("section", "dp", None),
        P("section", "dp", None),
    )
    return jax.shard_map(
        per_device,
        mesh=mesh,
        in_specs=placed,
        out_specs=(
            P("section", "dp", None),
            P("section", "dp", None),
            P("section", "dp", None),
            P("cuts", "section", "dp", None),
        ),
        check_vma=False,
    )
```

```python
import functools

import jax
import jax.numpy as jnp
from jax import lax
from jax.experimental import pallas as pl
from jax.experimental.pallas import tpu as pltpu
from jax.sharding import PartitionSpec as P

CAP = 64


def from_behind(block, axis, distance):
    devices = range(lax.axis_size(axis))
    route = [(i - distance, i) for i in devices if i - distance in devices]
    return lax.ppermute(block, axis, route)


def contract_last(left, right):
    return lax.dot_general(
        left, right, (((1,), (1,)), ((), ())), preferred_element_type=jnp.float32
    )


def contract_first(left, right):
    return lax.dot_general(
        left, right, (((0,), (0,)), ((), ())), preferred_element_type=jnp.float32
    )


def hidden_backward(rows_acts, rows_grads, gate_local, up_local, down_local):
    gate_pre = contract_last(rows_acts, gate_local)
    up_pre = contract_last(rows_acts, up_local)
    sig_gate = jax.nn.sigmoid(gate_pre)
    silu_gate = gate_pre * sig_gate
    hidden = (silu_gate * up_pre).astype(jnp.bfloat16)
    hidden_grad = contract_last(rows_grads, down_local)
    gate_grad = (hidden_grad * up_pre * sig_gate * (1.0 + gate_pre * (1.0 - sig_gate))).astype(
        jnp.bfloat16
    )
    up_grad = (hidden_grad * silu_gate).astype(jnp.bfloat16)
    return hidden, gate_grad, up_grad


TILES = 3
VMEM_BUDGET = 60 * 2**20


def exchange_kernel(
    n, acts_in, grads_in, gate_hbm, up_hbm, down_hbm,
    acts_out, grads_out, hidden_o, gate_o, up_o, part, next_up, next_down,
    acts_buf, grads_buf, gate_w, up_w, down_w, gate_t, up_t, gate_pre, up_pre,
    from_low, from_high, own_sem, weight_sem, out_sem, z_recv, up_send, down_send, x_recv, x_send,
    relay_send, low_recv, high_recv, sum_up_send, sum_down_send,
):
    i = lax.axis_index("dp")
    c = lax.axis_index("cuts")
    other = 1 - c
    cap = acts_in.shape[0]
    rows = n * cap
    hid, width = gate_w.shape
    tile = hid // TILES
    bufs = (acts_buf, grads_buf)
    has_low, has_high = i > 0, i < n - 1
    first, last = i == 0, i == n - 1
    second, next_last = i == 1, i == n - 2
    low, high, across = {"dp": i - 1}, {"dp": i + 1}, {"cuts": other}

    weight_copies = [
        pltpu.make_async_copy(src, dst, weight_sem.at[k])
        for k, (src, dst) in enumerate(
            ((gate_hbm, gate_w), (up_hbm, up_w), (down_hbm, down_w))
        )
    ]

    def slot(kind, replica, j):
        return bufs[kind].at[replica, pl.ds(pl.multiple_of(j * cap, cap), cap), :]

    own_copies = [
        pltpu.make_async_copy(src, slot(kind, c, i), own_sem.at[kind])
        for kind, src in enumerate((acts_in, grads_in))
    ]
    for copy in own_copies:
        copy.start()

    barrier = pltpu.get_barrier_semaphore()

    def greet(where):
        pl.semaphore_signal(
            barrier, inc=1, device_id=where, device_id_type=pl.DeviceIdType.MESH
        )

    pl.when(has_low)(lambda: greet(low))
    pl.when(has_high)(lambda: greet(high))
    greet(across)
    pl.semaphore_wait(barrier, 1 + jnp.int32(has_low) + jnp.int32(has_high))
    for copy in own_copies:
        copy.wait()

    def send(kind, j, where, send_sem, recv_sem):
        return pltpu.make_async_remote_copy(
            src_ref=slot(kind, c, j),
            dst_ref=slot(kind, c, j),
            send_sem=send_sem.at[kind, j],
            recv_sem=recv_sem.at[kind, j],
            device_id=where,
            device_id_type=pl.DeviceIdType.MESH,
        )

    def to_high(kind, j):
        return send(kind, j, high, up_send, z_recv)

    def to_low(kind, j):
        return send(kind, j, low, down_send, z_recv)

    def to_other(kind, j):
        return send(kind, j, across, x_send, x_recv)

    def from_other(kind, j):
        return pltpu.make_async_remote_copy(
            src_ref=slot(kind, other, j),
            dst_ref=slot(kind, other, j),
            send_sem=x_send.at[kind, j],
            recv_sem=x_recv.at[kind, j],
            device_id=across,
            device_id_type=pl.DeviceIdType.MESH,
        )

    def relay(kind, j, where):
        return pltpu.make_async_remote_copy(
            src_ref=slot(kind, other, j),
            dst_ref=slot(kind, other, j),
            send_sem=relay_send.at[kind],
            recv_sem=x_recv.at[kind, j],
            device_id=where,
            device_id_type=pl.DeviceIdType.MESH,
        )

    def crosses(kind, d):
        if d == 1:
            relayed = jnp.logical_or(second, last) if kind else second
            return jnp.logical_not(relayed)
        if d == -1:
            relayed = jnp.logical_or(next_last, first) if kind else next_last
            return jnp.logical_not(relayed)
        return i >= 0

    def prepare(replica, t):
        some = pl.ds(pl.multiple_of(t * tile, tile), tile)
        cols = pl.ds(pl.multiple_of(replica * rows, rows), rows)
        gate_pre[some, cols] = contract_last(gate_w[some, :], acts_buf[replica])
        up_pre[some, cols] = contract_last(up_w[some, :], acts_buf[replica])

    def finish(replica, t):
        some = pl.ds(pl.multiple_of(t * tile, tile), tile)
        cols = pl.ds(pl.multiple_of(replica * rows, rows), rows)
        hidden_grad = contract_last(down_w[some, :], grads_buf[replica])
        gate, up = gate_pre[some, cols], up_pre[some, cols]
        sig = jax.nn.sigmoid(gate)
        silu = gate * sig
        hidden_o[some, cols] = (silu * up).astype(jnp.bfloat16)
        gate_o[some, cols] = (
            hidden_grad * up * sig * (1.0 + gate * (1.0 - sig))
        ).astype(jnp.bfloat16)
        up_o[some, cols] = (hidden_grad * silu).astype(jnp.bfloat16)

    def receive(kind, d):
        @pl.when(i - d >= 0)
        def _():
            to_high(kind, i - d).wait_recv()
            pl.when(has_high)(lambda: to_high(kind, i - d).start())
            pl.when(crosses(kind, d))(lambda: to_other(kind, i - d).start())

        @pl.when(i + d < n)
        def _():
            to_low(kind, i + d).wait_recv()
            pl.when(has_low)(lambda: to_low(kind, i + d).start())
            pl.when(crosses(kind, -d))(lambda: to_other(kind, i + d).start())

    def relay_ends(kind):
        @pl.when(first)
        def _():
            from_other(kind, 0).wait_recv()
            relay(kind, 0, high).start()

        @pl.when(last)
        def _():
            from_other(kind, n - 1).wait_recv()
            relay(kind, n - 1, low).start()

    def await_other(kind, j):
        seen = []
        if j == 0:
            seen.append(first)
        if j == n - 1:
            seen.append(last)
        if kind == 1 and j == 1:
            seen.append(second)
        if kind == 1 and j == n - 2:
            seen.append(next_last)
        if seen:
            pl.when(jnp.logical_not(functools.reduce(jnp.logical_or, seen)))(
                lambda: from_other(kind, j).wait_recv()
            )
        else:
            from_other(kind, j).wait_recv()

    pl.when(has_high)(lambda: to_high(0, i).start())
    pl.when(has_low)(lambda: to_low(0, i).start())
    to_other(0, i).start()
    for copy in weight_copies:
        copy.start()
    for d in range(n):
        if d > 0:
            receive(0, d)
        if d == 1:
            relay_ends(0)
        pl.when(jnp.logical_and(has_high, i == d))(lambda: to_high(1, i).start())
        pl.when(jnp.logical_and(has_low, i == n - 1 - d))(lambda: to_low(1, i).start())
    to_other(1, i).start()
    for copy in weight_copies:
        copy.wait()

    todo = [(c, t) for t in range(TILES)] + [(other, t) for t in range(TILES)]
    for d in range(1, n):
        for _ in range(2):
            if todo:
                replica, t = todo.pop(0)
                if replica is other and t == 0:
                    for j in range(n):
                        await_other(0, j)
                prepare(replica, t)
        receive(1, d)
        if d == 2:
            relay_ends(1)
    for replica, t in todo:
        prepare(replica, t)

    @pl.loop(0, TILES)
    def _(t):
        finish(c, t)

    own_cols = pl.ds(pl.multiple_of(c * rows, rows), rows)
    gate_t[...] = jnp.transpose(gate_o[:, own_cols])
    up_t[...] = jnp.transpose(up_o[:, own_cols])
    step = 512

    @pl.loop(0, width // step)
    def _(t):
        some = pl.ds(pl.multiple_of(t * step, step), step)
        part[:, some] = (
            jnp.dot(gate_t[...], gate_w[:, some], preferred_element_type=jnp.float32)
            + jnp.dot(up_t[...], up_w[:, some], preferred_element_type=jnp.float32)
        ).astype(jnp.bfloat16)

    def share(j):
        return pl.ds(pl.multiple_of(j * cap, cap), cap)

    def sum_high():
        return pltpu.make_async_remote_copy(
            src_ref=part.at[share(n - 1), :],
            dst_ref=from_low,
            send_sem=sum_up_send,
            recv_sem=low_recv,
            device_id=high,
            device_id_type=pl.DeviceIdType.MESH,
        )

    def sum_low():
        return pltpu.make_async_remote_copy(
            src_ref=part.at[share(0), :],
            dst_ref=from_high,
            send_sem=sum_down_send,
            recv_sem=high_recv,
            device_id=low,
            device_id_type=pl.DeviceIdType.MESH,
        )

    pl.when(first)(lambda: sum_high().start())
    pl.when(last)(lambda: sum_low().start())

    @pl.when(second)
    def _():
        to_low(1, n - 1).wait_send()
        from_other(1, 1).wait_recv()
        relay(1, 1, low).start()

    @pl.when(next_last)
    def _():
        to_high(1, 0).wait_send()
        from_other(1, n - 2).wait_recv()
        relay(1, n - 2, high).start()

    for j in range(n):
        await_other(1, j)
    out_copies = [
        pltpu.make_async_copy(acts_buf, acts_out, out_sem.at[0]),
        pltpu.make_async_copy(grads_buf, grads_out, out_sem.at[1]),
    ]
    for copy in out_copies:
        copy.start()

    @pl.loop(0, TILES)
    def _(t):
        finish(other, t)

    next_up[...] = part[share(lax.rem(i + n - 2, n)), :]
    next_down[...] = part[share(lax.rem(i + 2, n)), :]

    @pl.when(second)
    def _():
        sum_high().wait_recv()
        next_up[...] = (
            next_up[...].astype(jnp.float32) + from_low[...].astype(jnp.float32)
        ).astype(jnp.bfloat16)

    @pl.when(next_last)
    def _():
        sum_low().wait_recv()
        next_down[...] = (
            next_down[...].astype(jnp.float32) + from_high[...].astype(jnp.float32)
        ).astype(jnp.bfloat16)

    pl.when(first)(lambda: sum_high().wait_send())
    pl.when(last)(lambda: sum_low().wait_send())

    @pl.when(first)
    def _():
        for kind in range(2):
            relay(kind, 0, high).wait_send()

    @pl.when(last)
    def _():
        for kind in range(2):
            relay(kind, n - 1, low).wait_send()

    pl.when(second)(lambda: relay(1, 1, low).wait_send())
    pl.when(next_last)(lambda: relay(1, n - 2, high).wait_send())
    for kind in range(2):
        to_other(kind, i).wait_send()
        pl.when(has_high)(lambda kind=kind: to_high(kind, i).wait_send())
        pl.when(has_low)(lambda kind=kind: to_low(kind, i).wait_send())
    for d in range(1, n):
        for kind in range(2):

            @pl.when(i - d >= 0)
            def _(kind=kind, d=d):
                early = jnp.logical_and(next_last, jnp.bool_(kind == 1 and d == n - 2))
                pl.when(jnp.logical_and(has_high, jnp.logical_not(early)))(
                    lambda: to_high(kind, i - d).wait_send()
                )
                pl.when(crosses(kind, d))(lambda: to_other(kind, i - d).wait_send())

            @pl.when(i + d < n)
            def _(kind=kind, d=d):
                early = jnp.logical_and(second, jnp.bool_(kind == 1 and d == n - 2))
                pl.when(jnp.logical_and(has_low, jnp.logical_not(early)))(
                    lambda: to_low(kind, i + d).wait_send()
                )
                pl.when(crosses(kind, -d))(lambda: to_other(kind, i + d).wait_send())

    for copy in out_copies:
        copy.wait()


def kernel_bytes(n, cap, hid, width):
    weights = 3 * hid * width * 2
    rows = 4 * n * cap * width * 2
    hidden = (6 + 2 + 8) * hid * n * cap * 2
    sums = 3 * n * cap * width * 2 + cap * width * 4
    return weights + rows + hidden + sums


def exchange(n, acts, grads, gate_local, up_local, down_local):
    cap, width = acts.shape
    hid = gate_local.shape[0]
    rows = n * cap
    bf16 = jnp.bfloat16
    both = jax.ShapeDtypeStruct((2, rows, width), bf16)
    units = jax.ShapeDtypeStruct((hid, 2 * rows), bf16)
    anywhere = pl.BlockSpec(memory_space=pl.ANY)
    vmem = pl.BlockSpec(memory_space=pltpu.VMEM)
    dma = pltpu.SemaphoreType.DMA
    return pl.pallas_call(
        functools.partial(exchange_kernel, n),
        out_shape=[both, both, units, units, units,
                   jax.ShapeDtypeStruct((rows, width), bf16),
                   jax.ShapeDtypeStruct((cap, width), bf16),
                   jax.ShapeDtypeStruct((cap, width), bf16)],
        in_specs=[anywhere] * 5,
        out_specs=[anywhere, anywhere] + [vmem] * 6,
        scratch_shapes=[
            pltpu.VMEM((2, rows, width), bf16),
            pltpu.VMEM((2, rows, width), bf16),
            pltpu.VMEM((hid, width), bf16),
            pltpu.VMEM((hid, width), bf16),
            pltpu.VMEM((hid, width), bf16),
            pltpu.VMEM((rows, hid), bf16),
            pltpu.VMEM((rows, hid), bf16),
            pltpu.VMEM((hid, 2 * rows), jnp.float32),
            pltpu.VMEM((hid, 2 * rows), jnp.float32),
            pltpu.VMEM((cap, width), bf16),
            pltpu.VMEM((cap, width), bf16),
            dma((2,)), dma((3,)), dma((2,)),
            dma((2, n)), dma((2, n)), dma((2, n)), dma((2, n)), dma((2, n)),
            dma((2,)), dma, dma, dma, dma,
        ],
        compiler_params=pltpu.CompilerParams(
            collective_id=0, has_side_effects=True, vmem_limit_bytes=VMEM_BUDGET
        ),
        cost_estimate=pl.CostEstimate(
            flops=16 * rows * hid * width, bytes_accessed=8 * hid * width, transcendentals=0
        ),
    )(acts, grads, gate_local, up_local, down_local)


def chained_sum(n, part, up, down):
    i = lax.axis_index("dp")
    sections = range(lax.axis_size("section"))
    shares = part.reshape(n, CAP, part.shape[1])

    def mine(j):
        return lax.dynamic_index_in_dim(shares, jnp.clip(j, 0, n - 1), keepdims=False)

    def hop(block, senders, step, back):
        pairs = [
            (s * n + k, (s - back) * n + k + step)
            for s in sections
            for k in senders
            if s >= back
        ]
        return lax.ppermute(block, ("section", "dp"), pairs)

    def joined(left, right):
        return (left.astype(jnp.float32) + right.astype(jnp.float32)).astype(jnp.bfloat16)

    for t in range(2, n):
        if t > 2:
            up = joined(up, mine(i + n - t))
            down = joined(down, mine(i - n + t))
        back = int(t == n - 1)
        up = hop(up, range(t), 1, back)
        down = hop(down, range(n - t, n), -1, back)
    own = hop(mine(i), range(n), 0, 1)
    total = own.astype(jnp.float32) + up.astype(jnp.float32) + down.astype(jnp.float32)
    return total.astype(jnp.bfloat16)


def per_device(
    activations, upstream_grad, routes, router_probs, gate_weight, up_weight, down_weight
):
    local_acts = activations[0, 0]
    local_grads = upstream_grad[0, 0]
    expert_hits = routes[0, 0] == 0
    router_weight = jnp.sum(jnp.where(expert_hits, router_probs[0, 0], jnp.float32(0.0)), axis=1)
    is_routed = jnp.any(expert_hits, axis=1)
    row_index = jnp.cumsum(is_routed.astype(jnp.int32)) - 1
    wanted = jnp.arange(CAP, dtype=jnp.int32)
    picker = ((row_index[None, :] == wanted[:, None]) & is_routed[None, :]).astype(jnp.bfloat16)
    scaled = (router_weight[:, None] * local_grads.astype(jnp.float32)).astype(jnp.bfloat16)
    packed_acts = jnp.dot(picker, local_acts, preferred_element_type=jnp.float32).astype(
        jnp.bfloat16
    )
    packed_grads = jnp.dot(picker, scaled, preferred_element_type=jnp.float32).astype(jnp.bfloat16)
    gate_local = gate_weight[0]
    up_local = up_weight[0]
    down_local = down_weight[0]
    n = lax.axis_size("dp")
    hid, width = gate_local.shape
    if kernel_bytes(n, CAP, hid, width) <= VMEM_BUDGET and hid % (16 * TILES) == 0 and n >= 4:
        acts, grads, hidden, gate_grad, up_grad, part, next_up, next_down = exchange(
            n, packed_acts, packed_grads, gate_local, up_local, down_local
        )
        behind_rows = chained_sum(n, part, next_up, next_down)
        both_acts = acts.reshape(2 * n * CAP, width)
        both_grads = grads.reshape(2 * n * CAP, width)
        summed = functools.partial(jnp.dot, preferred_element_type=jnp.float32)
    else:
        rows_acts = lax.all_gather(packed_acts, "dp", axis=0, tiled=True)
        rows_grads = lax.all_gather(packed_grads, "dp", axis=0, tiled=True)
        both_acts = lax.all_gather(rows_acts, "cuts", axis=0, tiled=True)
        both_grads = lax.all_gather(rows_grads, "cuts", axis=0, tiled=True)
        _, gate_grad, up_grad = hidden_backward(
            rows_acts, rows_grads, gate_local, up_local, down_local
        )
        input_rows = lax.psum_scatter(
            (
                jnp.dot(gate_grad, gate_local, preferred_element_type=jnp.float32)
                + jnp.dot(up_grad, up_local, preferred_element_type=jnp.float32)
            ).astype(jnp.bfloat16),
            "dp",
            scatter_dimension=0,
            tiled=True,
        )
        hidden, gate_grad, up_grad = hidden_backward(
            both_acts, both_grads, gate_local, up_local, down_local
        )
        behind_rows = from_behind(input_rows, "section", -1)
        summed = contract_first
    grad_gate = summed(gate_grad, both_acts).astype(jnp.bfloat16)[None]
    grad_up = summed(up_grad, both_acts).astype(jnp.bfloat16)[None]
    grad_down = summed(hidden, both_grads).astype(jnp.bfloat16)[None]
    slot = jnp.where(is_routed, row_index, -1).astype(jnp.bfloat16)
    behind_slot = from_behind(slot + 1.0, "section", -1) - 1.0
    behind_picker = (
        behind_slot[None, :].astype(jnp.int32) == wanted[:, None]
    ).astype(jnp.bfloat16)
    prev_grad = contract_first(behind_picker, behind_rows).astype(jnp.bfloat16)[None, None]
    return (grad_gate, grad_up, grad_down, prev_grad)


def solution(mesh):
    placed = (
        P("cuts", "section", "dp", None),
        P("cuts", "section", "dp", None),
        P("cuts", "section", "dp", None),
        P("cuts", "section", "dp", None),
        P("section", "dp", None),
        P("section", "dp", None),
        P("section", "dp", None),
    )
    return jax.shard_map(
        per_device,
        mesh=mesh,
        in_specs=placed,
        out_specs=(
            P("section", "dp", None),
            P("section", "dp", None),
            P("section", "dp", None),
            P("cuts", "section", "dp", None),
        ),
        check_vma=False,
    )
```
